32 devices in a mesh: ep: 16 (over z, y, core), tp: 2 (over x).
Axes of the slice: x: 2, y: 2, z: 4, core: 2. Of those that a mesh axis runs over, the one named last changes fastest.
Arguments:
- tokens_in: bfloat16 [16384, 1536], P('ep'), may hold values from -12 to 12
- lengths: int32 [16], P('ep'), may hold values from 1 to 1024, 8192 in all
- attn_gain: float32 [1536], replicated, may hold values from 0.1 to 1.9
- q_proj: float32 [1536, 1536], P('ep', 'tp'), may hold values from -2 to 2
- k_proj: float32 [1536, 512], P('ep', 'tp'), may hold values from -2 to 2
- value_projection: float32 [1536, 512], P('ep', 'tp'), may hold values from -0.15625 to 0.15625
- o_proj: float32 [1536, 1536], P('tp', 'ep'), may hold values from -2.5 to 2.5
- key_value_pages: bfloat16 [128, 16, 1024], P('ep', None, 'tp'), may hold values from -6 to 6
- page_table: int32 [16, 16, 2], P(None, 'ep'), may hold values from 0 to 7
- moe_gain: float32 [1536], replicated, may hold values from 0.1 to 1.9
- router: bfloat16 [1536, 16], replicated, may hold values from -5 to 5
- expert_ids: int32 [16384, 8], P(('ep', 'tp')), may hold values from 0 to 15, all different within a row; in each aligned block of 512 rows (0 to 511, 512 to 1023, ...) at most 384 rows name the same one
- gate_up_proj: float32 [16, 1536, 1024], P('ep', 'tp'), may hold values from -0.15625 to 0.15625
- down_proj: float32 [16, 512, 1536], P('ep', 'tp'), may hold values from -0.25 to 0.25
Outputs:
- layer_out: bfloat16 [16384, 1536], P(('ep', 'tp'))
The draws below stay inside these ranges and needn't reach their ends.
Inputs may be any that keep to these rules, and one draw needn't show every extreme that they name: `expert_ids`: among the 512 token slots of each aligned block (one device's slots), no expert is named more than 384 times, a bound that some block reaches. `lengths`: some prompt is 1024 tokens long.
All inputs are finite; a program needn't handle non-finite values. No bound on the sum of `lengths` on one device may be relied on, other than what follows from the above.
Results may differ from the reference program's by a relative error of at most 0.018.
Values may be sent and summed in bfloat16 or wider, within the bound.
A program may use at most 192 MiB of HBM per device.

```python
import math
import jax
import jax.numpy as jnp
import numpy as np
from jax import lax

MODEL_DIM = 1536
QUERY_HEADS = 24
KEY_VALUE_HEADS = 8
HEAD_WIDTH = 64
FF = 512
TOPK = 8
PROMPT_SLOTS = 1024
PAGE_TOKENS = 16
SLOTS = 2
POOL_PAGES = 8
EXPERTS = 16
PROMPTS = 16
TOKENS = 16384
ROWS = 512
CAP = 384
N_EP = 16
N_TP = 2


def draw_tokens_in(key, part):
    draw_sample = jax.random.truncated_normal(jax.random.fold_in(key, 1), -6.0, 6.0, (TOKENS, MODEL_DIM), jnp.float32)
    return draw_sample.astype(jnp.bfloat16)


def draw_q_proj(key, part):
    draw_sample = jax.random.truncated_normal(jax.random.fold_in(key, 11), -6.0, 6.0, (MODEL_DIM, QUERY_HEADS * HEAD_WIDTH), jnp.float32) * MODEL_DIM ** (-0.5)
    return draw_sample


def draw_k_proj(key, part):
    draw_sample = jax.random.truncated_normal(jax.random.fold_in(key, 21), -6.0, 6.0, (MODEL_DIM, KEY_VALUE_HEADS * HEAD_WIDTH), jnp.float32) * MODEL_DIM ** (-0.5)
    return draw_sample


def draw_router(key, part):
    draw_sample = jax.random.truncated_normal(jax.random.fold_in(key, 31), -6.0, 6.0, (MODEL_DIM, EXPERTS), jnp.float32) * MODEL_DIM ** (-0.5)
    return draw_sample.astype(jnp.bfloat16)


def place_ends(entries, rng, least, largest):
    spot = [jax.random.randint(jax.random.fold_in(rng, axis), (), 0, length) for axis, length in enumerate(entries.shape)]
    widest = entries.shape.index(max(entries.shape))
    neighbour = spot[:widest] + [(spot[widest] + 1) % entries.shape[widest]] + spot[widest + 1:]
    return entries.at[tuple(spot)].set(least).at[tuple(neighbour)].set(largest)


def steps_of(rng, dims, shards, low, top_value):
    loudness, own = 1.0, jax.random.fold_in(rng, 6)
    for axis_at, blocks in shards:
        heights = jnp.exp(jax.random.uniform(jax.random.fold_in(own, axis_at), (blocks,), jnp.float32, low / len(shards), top_value / len(shards)))
        loudness = loudness * jnp.repeat(heights, dims[axis_at] // blocks).reshape([-1 if axis == axis_at else 1 for axis in range(len(dims))])
    return loudness


def length_profile(count, total, most, lean):
    portions = [(1 << 20) // math.isqrt(standing ** lean) + 1 for standing in range(2, count + 1)]
    rest, given = total - most - (count - 1), [1] * (count - 1)
    while rest > 0:
        movable = [i for i in range(count - 1) if given[i] < most]
        mass, budget = sum([portions[i] for i in movable]), rest
        for i in movable:
            addition = min(most - given[i], max(1, budget * portions[i] // mass), rest)
            given[i] = given[i] + addition
            rest = rest - addition
    return np.array([most] + given)


def ragged(own_key, count, total, bound, slope):
    if count == 2:
        one = jax.random.randint(own_key, (), max(1, total - bound), min(bound, total - 1) + 1)
        return jnp.stack([one, total - one])
    sizes = jnp.asarray(length_profile(count, total, bound, slope), jnp.int32)
    couples = (count - 1) // 2
    source_of, receiver = sizes[1:1 + 2 * couples:2], sizes[2:2 + 2 * couples:2]
    slack = jnp.minimum(source_of - 1, bound - receiver)
    passed = jax.random.randint(jax.random.fold_in(own_key, 1), (couples,), 0, 1 << 20) % (slack + 1)
    sizes = sizes.at[1:1 + 2 * couples:2].set(source_of - passed).at[2:2 + 2 * couples:2].set(receiver + passed)
    return sizes[jax.random.permutation(jax.random.fold_in(own_key, 2), count)]


def shared_out(key, own, number, rows, amount, top, bound, lean):
    sequence = jax.random.permutation(key, amount)
    crowded, usual = shares(amount, rows * top, bound, lean, True), shares(amount, rows * top, bound, lean, False)
    places = jnp.arange(amount)

    def named(tallies, rotation):
        used = int((tallies > 0).sum())
        fixed = max(1, used // 4)
        passed = fixed + (places - fixed + rotation * (used - fixed)) % max(1, amount - fixed)
        return jnp.zeros((amount,), jnp.int32).at[sequence[jnp.where(places < fixed, places, passed)]].set(jnp.asarray(tallies, jnp.int32))

    tallies = jnp.where(number % 4 == 0, named(crowded, number // 4), named(usual, number - number // 4 - 1))
    mixed = jax.random.permutation(jax.random.fold_in(own, 3), amount)
    source_of, taker = mixed[0:amount // 2 * 2:2], mixed[1:amount // 2 * 2:2]
    slack = jnp.minimum(tallies[source_of] - 1, bound - tallies[taker]) // 2
    slack = jnp.where((source_of == sequence[0]) | (taker == sequence[0]) | (tallies[taker] == 0), 0, jnp.maximum(slack, 0))
    passed = jax.random.randint(jax.random.fold_in(own, 4), (amount // 2,), 0, 1 << 20) % (slack + 1)
    tallies = tallies.at[source_of].add(-passed).at[taker].add(passed)
    members = jnp.searchsorted(jnp.cumsum(tallies), jnp.arange(rows * top), side="right").astype(jnp.int32)
    grid = members.reshape(top, rows).T
    grid = grid[jax.random.permutation(jax.random.fold_in(own, 1), rows)]
    rotation = jax.random.randint(jax.random.fold_in(own, 2), (rows, 1), 0, top)
    return jnp.take_along_axis(grid, (jnp.arange(top)[None, :] + rotation) % top, axis=1)


def shares(amount, total, reach, skew, full):
    portions = [(1 << 20) // math.isqrt(grade ** skew) + 1 for grade in range(1, amount + 1)]
    largest = reach if full else min(reach, max(-(-total // amount), total * portions[0] // sum(portions)))
    least = 1 if total - largest >= amount - 1 else 0
    holding, rest = [largest] + [least] * (amount - 1), total - largest - least * (amount - 1)
    while rest > 0:
        candidates = [i for i in range(1, amount) if holding[i] < largest] or [i for i in range(1, amount) if holding[i] < reach]
        mass, budget = sum([portions[i] for i in candidates]), rest
        for i in candidates:
            more = min(reach - holding[i], max(1, budget * portions[i] // mass), rest)
            holding[i] = holding[i] + more
            rest = rest - more
    return np.array(holding)


def noise(key, shape, deviation, most, pieces=(), kind=jnp.bfloat16):
    loudness = steps_of(key, shape, pieces, -0.22, 0.18) if pieces else 1.0
    values = jax.random.normal(key, shape, jnp.float32) * deviation * loudness
    return jnp.minimum(jnp.maximum(values, -most), most).astype(kind)


def setup_inputs(seed: int = 0) -> dict:
    key_list = jax.random.split(jax.random.key(seed), 15)
    tokens_in = draw_tokens_in(jax.random.fold_in(key_list[14], 71), 0)
    lengths = ragged(key_list[1], PROMPTS, PROMPTS * PROMPT_SLOTS // 2, PROMPT_SLOTS, 2).astype(jnp.int32)
    attn_gain = jnp.clip(1.0 + 0.18 * jax.random.normal(key_list[2], (MODEL_DIM,), jnp.float32), 0.1, 1.9)
    q_proj = draw_q_proj(jax.random.fold_in(key_list[14], 71), 0)
    k_proj = draw_k_proj(jax.random.fold_in(key_list[14], 71), 0)
    value_projection = noise(key_list[5], (MODEL_DIM, KEY_VALUE_HEADS * HEAD_WIDTH), MODEL_DIM ** -0.5, 0.15625, ((0, 16), (1, 2)), jnp.float32)
    o_proj = noise(key_list[6], (QUERY_HEADS * HEAD_WIDTH, MODEL_DIM), 0.25, 2.5, ((0, 2), (1, 16)), jnp.float32)
    key_value_pages = noise(key_list[7], (N_EP * POOL_PAGES, PAGE_TOKENS, KEY_VALUE_HEADS * 2 * HEAD_WIDTH), 1.0, 6.0, ((0, 16), (2, 2)))
    page_table = place_ends(jax.random.randint(key_list[8], (PROMPTS, N_EP, SLOTS), 0, POOL_PAGES), jax.random.fold_in(key_list[8], 1), 0, POOL_PAGES - 1).astype(jnp.int32)
    moe_gain = jnp.clip(1.0 + 0.18 * jax.random.normal(key_list[9], (MODEL_DIM,), jnp.float32), 0.1, 1.9)
    router = draw_router(jax.random.fold_in(key_list[14], 71), 0)
    expert_ids_keys = jax.random.split(jax.random.fold_in(key_list[11], 1), TOKENS // ROWS)
    expert_ids_turns = jax.random.permutation(jax.random.fold_in(key_list[11], 3), TOKENS // ROWS)
    expert_ids = jax.vmap(lambda own, number: shared_out(jax.random.fold_in(key_list[11], 2), own, number, ROWS, EXPERTS, TOPK, CAP, 2))(expert_ids_keys, expert_ids_turns).reshape((TOKENS, TOPK))
    gate_up_proj = noise(key_list[12], (EXPERTS, MODEL_DIM, 2 * FF), MODEL_DIM ** -0.5, 0.15625, ((0, 16), (1, 2)), jnp.float32)
    down_proj = noise(key_list[13], (EXPERTS, FF, MODEL_DIM), FF ** -0.5, 0.25, ((0, 16), (1, 2)), jnp.float32)
    return {"tokens_in": tokens_in, "lengths": lengths, "attn_gain": attn_gain, "q_proj": q_proj, "k_proj": k_proj, "value_projection": value_projection, "o_proj": o_proj, "key_value_pages": key_value_pages, "page_table": page_table, "moe_gain": moe_gain, "router": router, "expert_ids": expert_ids, "gate_up_proj": gate_up_proj, "down_proj": down_proj}


epsilon = 1e-05

def rms_scale(values, norm_gain):
    mean_square = lax.optimization_barrier(jnp.mean(values * values, axis=-1, keepdims=True))
    return values * lax.rsqrt(mean_square + epsilon) * norm_gain

def apply_rotary(vectors, token_positions):
    half_width = vectors.shape[-1] // 2
    frequency = jnp.exp(jnp.arange(half_width, dtype=jnp.float32) * (-2.0 * math.log(10000.0) / vectors.shape[-1]))
    angles = token_positions.astype(jnp.float32)[:, None] * frequency[None, :]
    cosine = jnp.cos(angles)[:, None, :]
    sine_table = jnp.sin(angles)[:, None, :]
    first_half = vectors[..., :half_width]
    second_half = vectors[..., half_width:]
    return jnp.concatenate([first_half * cosine - second_half * sine_table, second_half * cosine + first_half * sine_table], axis=-1)

def reference(tokens_in, lengths, attn_gain, q_proj, k_proj, value_projection, o_proj, key_value_pages, page_table, moe_gain, router, expert_ids, gate_up_proj, down_proj):
    query_weight = q_proj.astype(jnp.bfloat16)
    key_matrix = k_proj.astype(jnp.bfloat16)
    value_matrix = value_projection.astype(jnp.bfloat16)
    output_weight = o_proj.astype(jnp.bfloat16)
    prefix_length = N_EP * SLOTS * PAGE_TOKENS
    heads_per_group = QUERY_HEADS // KEY_VALUE_HEADS
    group_width = QUERY_HEADS * HEAD_WIDTH // N_TP
    pooled_page_count = key_value_pages.reshape(N_EP, POOL_PAGES, PAGE_TOKENS, KEY_VALUE_HEADS, 2, HEAD_WIDTH)
    token_positions = prefix_length + jnp.arange(PROMPT_SLOTS)
    key_pos = jnp.arange(prefix_length + PROMPT_SLOTS)
    query_pos = jnp.arange(PROMPT_SLOTS)
    source_pages = jnp.arange(N_EP)
    grouped_out = output_weight.reshape(N_TP, group_width, MODEL_DIM).astype(jnp.float32)

    def one_prompt(inputs):
        rows, length_here, lookup_table = inputs
        normalized_input = rms_scale(rows.astype(jnp.float32), attn_gain).astype(jnp.bfloat16)
        query_rows = apply_rotary(jnp.dot(normalized_input, query_weight, preferred_element_type=jnp.float32).reshape(PROMPT_SLOTS, QUERY_HEADS, HEAD_WIDTH), token_positions).astype(jnp.bfloat16)
        fresh_keys = apply_rotary(jnp.dot(normalized_input, key_matrix, preferred_element_type=jnp.float32).reshape(PROMPT_SLOTS, KEY_VALUE_HEADS, HEAD_WIDTH), token_positions).astype(jnp.bfloat16)
        fresh_values = jnp.dot(normalized_input, value_matrix, preferred_element_type=jnp.float32).reshape(PROMPT_SLOTS, KEY_VALUE_HEADS, HEAD_WIDTH).astype(jnp.bfloat16)
        page_list = pooled_page_count[source_pages[:, None], lookup_table].reshape(prefix_length, KEY_VALUE_HEADS, 2, HEAD_WIDTH)
        all_keys = jnp.concatenate([page_list[:, :, 0], fresh_keys], 0).astype(jnp.float32).transpose(1, 0, 2)
        all_values = jnp.concatenate([page_list[:, :, 1], fresh_values], 0).astype(jnp.float32).transpose(1, 0, 2)
        own = key_pos[None, :] - prefix_length
        allowed = (own < 0) | (own <= query_pos[:, None]) & (own < length_here)
        grouped_queries = query_rows.reshape(PROMPT_SLOTS, KEY_VALUE_HEADS, heads_per_group, HEAD_WIDTH).astype(jnp.float32).transpose(1, 2, 0, 3)

        def one_head(head_inputs):
            query_group, keys_here, values_here = head_inputs
            scores = jnp.einsum('gqd,kd->gqk', query_group, keys_here) * HEAD_WIDTH ** (-0.5)
            scores = jnp.where(allowed[None], scores, -1e+30)
            top_score = lax.optimization_barrier(jnp.max(scores, axis=-1, keepdims=True))
            weights = jnp.exp(scores - top_score)
            probs = (weights / lax.optimization_barrier(jnp.sum(weights, axis=-1, keepdims=True))).astype(jnp.bfloat16)
            return jnp.einsum('gqk,kd->gqd', probs.astype(jnp.float32), values_here).astype(jnp.bfloat16)
        heads_out = lax.map(one_head, (grouped_queries, all_keys, all_values))
        attended = heads_out.transpose(2, 0, 1, 3).reshape(PROMPT_SLOTS, QUERY_HEADS * HEAD_WIDTH)
        parts = jnp.einsum('lgw,gwd->gld', attended.reshape(PROMPT_SLOTS, N_TP, group_width).astype(jnp.float32), grouped_out)
        parts = lax.optimization_barrier(parts.astype(jnp.bfloat16)).astype(jnp.float32)
        return rows.astype(jnp.float32) + lax.optimization_barrier(jnp.sum(parts, axis=0))
    hidden = lax.map(one_prompt, (tokens_in.reshape(PROMPTS, PROMPT_SLOTS, MODEL_DIM), lengths, page_table)).reshape(TOKENS, MODEL_DIM)
    moe_in = rms_scale(hidden, moe_gain).astype(jnp.bfloat16)
    logits = jnp.dot(moe_in, router, preferred_element_type=jnp.float32)
    picked = jnp.take_along_axis(logits, expert_ids, axis=1)
    top_logit = lax.optimization_barrier(jnp.max(picked, axis=-1, keepdims=True))
    raised = jnp.exp(picked - top_logit)
    gates = raised / lax.optimization_barrier(jnp.sum(raised, axis=-1, keepdims=True))
    flat_ids = expert_ids.reshape(-1)
    flat_gates = gates.reshape(-1)
    order = jnp.argsort(flat_ids, stable=True).astype(jnp.int32)
    counts = lax.optimization_barrier(jnp.sum((flat_ids[:, None] == jnp.arange(EXPERTS)[None, :]).astype(jnp.int32), axis=0))
    starts = (jnp.cumsum(counts) - counts).astype(jnp.int32)
    most_rows = TOKENS // ROWS * CAP
    padded_order = jnp.concatenate([order, jnp.zeros((most_rows,), jnp.int32)])
    gate_up_all = gate_up_proj.astype(jnp.bfloat16)
    down_all = down_proj.astype(jnp.bfloat16)

    def one_expert(mixed, expert_inputs):
        gate_up_weight, down_weight, start, count = expert_inputs
        picks = lax.dynamic_slice_in_dim(padded_order, start.astype(jnp.int32), most_rows)
        live = jnp.arange(most_rows) < count
        token_index = picks // TOPK
        rows = moe_in[token_index]
        gate_up = jnp.dot(rows, gate_up_weight, preferred_element_type=jnp.float32)
        activated = (jax.nn.silu(gate_up[:, :FF]) * gate_up[:, FF:]).astype(jnp.bfloat16)
        expert_out = jnp.dot(activated, down_weight, preferred_element_type=jnp.float32).astype(jnp.bfloat16)
        weight_rows = jnp.where(live, flat_gates[picks], 0.0)
        return (mixed.at[token_index].add(expert_out.astype(jnp.float32) * weight_rows[:, None]), None)
    mixed, unused = lax.scan(one_expert, jnp.zeros((TOKENS, MODEL_DIM), jnp.float32), (gate_up_all, down_all, starts, counts))
    slot_index = jnp.arange(TOKENS)
    valid = slot_index % PROMPT_SLOTS < lengths[slot_index // PROMPT_SLOTS]
    return jnp.where(valid[:, None], hidden + mixed, 0.0).astype(jnp.bfloat16)
```

```python
import math

import jax
import jax.numpy as jnp
from jax import lax
from jax.sharding import PartitionSpec as P

QUERY_HEADS = 24
KEY_VALUE_HEADS = 8
HEAD_WIDTH = 64
FF = 512


epsilon = 1e-05


def rms_scale(values, norm_gain):
    mean_square = jnp.mean(values * values, axis=-1, keepdims=True)
    return values * lax.rsqrt(mean_square + epsilon) * norm_gain


def apply_rotary(vectors, token_positions):
    half_width = vectors.shape[-1] // 2
    frequency = jnp.exp(
        jnp.arange(half_width, dtype=jnp.float32) * (-2.0 * math.log(10000.0) / vectors.shape[-1])
    )
    angles = token_positions.astype(jnp.float32)[:, None] * frequency[None, :]
    cosine = jnp.cos(angles)[:, None, :]
    sine_table = jnp.sin(angles)[:, None, :]
    first_half = vectors[..., :half_width]
    second_half = vectors[..., half_width:]
    return jnp.concatenate(
        [
            first_half * cosine - second_half * sine_table,
            second_half * cosine + first_half * sine_table,
        ],
        axis=-1,
    )


def on_device(
    tokens_in,
    lengths,
    attn_gain,
    q_proj,
    k_proj,
    value_projection,
    o_proj,
    key_value_pages,
    page_table,
    moe_gain,
    router,
    expert_ids,
    gate_up_proj,
    down_proj,
):
    seq_len, model_width = tokens_in.shape
    tp_index = lax.axis_index("tp")
    heads_per_group = QUERY_HEADS // KEY_VALUE_HEADS
    kv_local = key_value_pages.shape[2] // (2 * HEAD_WIDTH)
    query_local = q_proj.shape[1] // HEAD_WIDTH
    query_width = q_proj.shape[1]
    kv_width = k_proj.shape[1]
    qkv_weight = lax.all_gather(
        jnp.concatenate([q_proj, k_proj, value_projection], axis=1).astype(jnp.bfloat16),
        "ep",
        axis=0,
        tiled=True,
    )
    output_weight = lax.all_gather(o_proj.T.astype(jnp.bfloat16), "ep", axis=0, tiled=True)
    gate_up_full, down_full = (
        lax.all_gather(gate_up_proj.astype(jnp.bfloat16), "tp", axis=1, tiled=True),
        lax.all_gather(down_proj.astype(jnp.bfloat16), "tp", axis=1, tiled=True),
    )
    chosen_pages = key_value_pages[page_table[:, 0, :]]
    arrived = lax.all_to_all(chosen_pages, "ep", split_axis=0, concat_axis=0, tiled=True)
    prefix_length = arrived.shape[0] * arrived.shape[1] * arrived.shape[2]
    prefix = arrived.reshape(prefix_length, kv_local, 2, HEAD_WIDTH)
    normalized_input = rms_scale(tokens_in.astype(jnp.float32), attn_gain).astype(jnp.bfloat16)
    token_positions = prefix_length + jnp.arange(seq_len)
    qkv = jnp.dot(normalized_input, qkv_weight, preferred_element_type=jnp.float32)
    rotated = apply_rotary(
        qkv[:, : query_width + kv_width].reshape(seq_len, query_local + kv_local, HEAD_WIDTH),
        token_positions,
    ).astype(jnp.bfloat16)
    query_rows = rotated[:, :query_local]
    fresh_keys = rotated[:, query_local:]
    fresh_values = (
        qkv[:, query_width + kv_width :].reshape(seq_len, kv_local, HEAD_WIDTH).astype(jnp.bfloat16)
    )
    length_here = lengths[0]
    own = jnp.arange(prefix_length + seq_len)[None, :] - prefix_length
    block_rows = min(256, seq_len)
    head_outputs = []
    for kv_index in range(kv_local):
        all_keys = jnp.concatenate([prefix[:, kv_index, 0], fresh_keys[:, kv_index]], 0)
        all_values = jnp.concatenate([prefix[:, kv_index, 1], fresh_values[:, kv_index]], 0)
        grouped_queries = query_rows[
            :, kv_index * heads_per_group : (kv_index + 1) * heads_per_group
        ].transpose(1, 0, 2)
        blocks = []
        for block_start in range(0, seq_len, block_rows):
            query_block = grouped_queries[:, block_start : block_start + block_rows]
            key_count = prefix_length + block_start + block_rows
            scores = jnp.einsum(
                "gqd,kd->gqk", query_block, all_keys[:key_count], preferred_element_type=jnp.float32
            ) * HEAD_WIDTH ** (-0.5)
            query_pos = block_start + jnp.arange(block_rows)
            own_here = own[:, :key_count]
            allowed = (own_here < 0) | (own_here <= query_pos[:, None]) & (own_here < length_here)
            scores = jnp.where(allowed[None], scores, -1e30)
            top_score = jnp.max(scores, axis=-1, keepdims=True)
            weights = jnp.exp(scores - top_score)
            total = jnp.sum(weights, axis=-1, keepdims=True)
            mixed_values = jnp.einsum(
                "gqk,kd->gqd",
                weights.astype(jnp.bfloat16),
                all_values[:key_count],
                preferred_element_type=jnp.float32,
            )
            blocks.append((mixed_values / total).astype(jnp.bfloat16))
        head_outputs.append(jnp.concatenate(blocks, axis=1))
    attended = (
        jnp.concatenate(head_outputs, axis=0)
        .transpose(1, 0, 2)
        .reshape(seq_len, query_local * HEAD_WIDTH)
    )
    partial_out = lax.dot_general(
        attended, output_weight, (((1,), (1,)), ((), ())), preferred_element_type=jnp.float32
    )
    attn_sum = lax.psum_scatter(
        partial_out.astype(jnp.bfloat16), "tp", scatter_dimension=0, tiled=True
    ).astype(jnp.float32)
    row_count = attn_sum.shape[0]
    own_rows = lax.dynamic_slice_in_dim(tokens_in, tp_index * row_count, row_count, 0)
    hidden = own_rows.astype(jnp.float32) + attn_sum
    moe_in = rms_scale(hidden, moe_gain).astype(jnp.bfloat16)
    expert_count = router.shape[1]
    logits = jnp.dot(moe_in, router, preferred_element_type=jnp.float32)
    expert_range = jnp.arange(expert_count)
    matches = expert_ids[:, :, None] == expert_range[None, None, :]
    picked = jnp.sum(jnp.where(matches, logits[:, None, :], 0.0), axis=-1)
    top_logit = jnp.max(picked, axis=-1, keepdims=True)
    raised = jnp.exp(picked - top_logit)
    gates = raised / jnp.sum(raised, axis=-1, keepdims=True)
    gate_table = jnp.sum(jnp.where(matches, gates[:, :, None], 0.0), axis=1).T
    exp_local = gate_up_proj.shape[0]
    first_expert = lax.axis_index("ep") * exp_local
    chunk_count = 2
    chunk_rows = row_count // chunk_count
    gathered = [
        lax.all_gather(moe_in[c * chunk_rows : (c + 1) * chunk_rows], "ep", axis=0, tiled=True)
        for c in range(chunk_count)
    ]
    all_gates = lax.all_gather(gate_table, "ep", axis=0)
    own_gates = lax.dynamic_slice_in_dim(all_gates, first_expert, exp_local, 1)
    mixed_parts = []
    for c in range(chunk_count):
        rows = gathered[c]
        chunk_gates = own_gates[:, :, c * chunk_rows : (c + 1) * chunk_rows]
        weighted = 0.0
        for e in range(exp_local):
            gate_up = jnp.dot(rows, gate_up_full[e], preferred_element_type=jnp.float32)
            activated = (jax.nn.silu(gate_up[:, :FF]) * gate_up[:, FF:]).astype(jnp.bfloat16)
            expert_out = jnp.dot(activated, down_full[e], preferred_element_type=jnp.float32)
            weighted = weighted + expert_out * chunk_gates[:, e].reshape(-1)[:, None]
        mixed_parts.append(
            lax.psum_scatter(
                weighted.astype(jnp.bfloat16), "ep", scatter_dimension=0, tiled=True
            ).astype(jnp.float32)
        )
    mixed = jnp.concatenate(mixed_parts, axis=0)
    valid = tp_index * row_count + jnp.arange(row_count) < length_here
    return jnp.where(valid[:, None], hidden + mixed, 0.0).astype(jnp.bfloat16)


def solution(mesh):
    in_specs = (
        P("ep", None),
        P("ep"),
        P(),
        P("ep", "tp"),
        P("ep", "tp"),
        P("ep", "tp"),
        P("tp", "ep"),
        P("ep", None, "tp"),
        P(None, "ep", None),
        P(),
        P(),
        P(("ep", "tp"), None),
        P("ep", "tp", None),
        P("ep", "tp", None),
    )
    out_specs = P(("ep", "tp"), None)
    return jax.shard_map(
        on_device, mesh=mesh, in_specs=in_specs, out_specs=out_specs, check_vma=False
    )
```
